32 devices in a mesh: groups: 2 (over y), row: 16 (over z, x, core).
Axes of the slice: x: 2, y: 2, z: 4, core: 2. Of those that a mesh axis runs over, the one named last changes fastest.
Arguments:
- features: bfloat16 [32768, 256], P(('groups', 'row')), parts along dimension 0, may hold values from -6 to 6
- tile_values: bfloat16 [2048, 128, 128], P(('groups', 'row')), parts along dimension 0, may hold values from -0.16992188 to 0.16992188
- tile_rows: int32 [2048], P(('groups', 'row')), parts along dimension 0, may hold values from -1 to 7, as said below
- tile_cols: int32 [2048], P(('groups', 'row')), parts along dimension 0, may hold values from 0 to 127, as said below
- bias: float32 [256], replicated, may hold values from -3 to 3
- weight: bfloat16 [256, 256], replicated, may hold values from -0.375 to 0.375
- cotangent: bfloat16 [32768, 256], P(('groups', 'row')), parts along dimension 0, may hold values from -6 to 6
Outputs:
- hidden: bfloat16 [32768, 256], P(('groups', 'row')), parts along dimension 0
- grad_features: bfloat16 [32768, 256], P(('groups', 'row')), parts along dimension 0
- grad_weight: float32 [512, 256], P('groups'), parts along dimension 0
- grad_bias: float32 [512], P('groups'), parts along dimension 0
The draws below stay inside these ranges and needn't reach their ends.
There are 2 independent parts, one for each index of `groups`. The reference program is written for one: setup_inputs(seed, part) draws one part's arguments, and reference() takes and returns one part's arrays. A program takes and returns all parts, laid end to end along the dimension named above; an argument that names none is the same for every part. Nothing has to cross between parts.
Inputs may be any that keep to these rules, and one draw needn't show every extreme that they name: `tile_rows`: row block of a slot's tile among its device's 8 row blocks, or -1 for an unused slot. A device's used slots come first; in every draw some device uses all 64 slots. `tile_cols`: for slots of the device holding row blocks d * 8 onward, the column block lies among the blocks of devices d - 1, d and d + 1 that exist in the slab.
All inputs are finite; a program needn't handle non-finite values.
Results may differ from the reference program's by a relative error of at most 0.0055.
The reference program's roundings to bfloat16 on the way count: a program that leaves them out, or rounds other values in their place, can miss the bound.
Values may be sent and summed in bfloat16 or wider, within the bound.
A program may use at most 64 MiB of HBM per device.

```python
import jax
import jax.numpy as jnp
from jax import lax

HID = 256
BLK = 128
NB_DEV = 8
TILE_DEV = 64
NODES = 16384
TILES = 1024
N_ROW = 16


def draw_tile_rows(key, part):
    key = jax.random.fold_in(key, 11)
    keys = jax.random.split(key, 4)
    devices = TILES // TILE_DEV
    live = jax.random.randint(keys[0], (devices,), TILE_DEV // 4, TILE_DEV + 1)
    fullest = jax.random.randint(keys[1], (), 0, devices)
    live = jnp.where(jnp.arange(devices) == fullest, TILE_DEV, live)
    upper = jax.random.randint(keys[2], (devices, TILE_DEV), 1, NB_DEV + 1)
    picked = jax.random.randint(keys[3], (devices, TILE_DEV), 0, 1 << 20) % upper
    slots = jnp.arange(TILE_DEV)[None, :]
    rows = jnp.where(slots < live[:, None], picked, -1)
    return rows.reshape(TILES).astype(jnp.int32)


def draw_tile_cols(key, part):
    key = jax.random.fold_in(key, 23)
    devices = TILES // TILE_DEV
    nblk = NB_DEV * devices
    owner = jnp.arange(devices)[:, None]
    lower = jnp.maximum(0, (owner - 1) * NB_DEV)
    upper = jnp.minimum(nblk, (owner + 2) * NB_DEV)
    drawn = jax.random.randint(key, (devices, TILE_DEV), 0, 1 << 20)
    cols = lower + drawn % (upper - lower)
    return cols.reshape(TILES).astype(jnp.int32)


def level_of(rng, dims, pieces, smallest, high):
    level = 1.0
    for axis_at, blocks in pieces:
        steps = jax.random.uniform(jax.random.fold_in(jax.random.fold_in(rng, 6), axis_at), (blocks,), jnp.float32, smallest / len(pieces), high / len(pieces))
        level = level * jnp.repeat(jnp.exp(steps), dims[axis_at] // blocks).reshape((-1,) + (1,) * (len(dims) - 1 - axis_at))
    return level


def centred(stream_key, dims, width, limit, shards=(), held_as=jnp.bfloat16):
    values = width * jax.random.normal(stream_key, dims, jnp.float32)
    if shards:
        values = values * level_of(stream_key, dims, shards, -0.22, 0.18)
    return jnp.clip(values, -limit, limit).astype(held_as)


def setup_inputs(seed: int = 0, part: int = 0) -> dict:
    streams_of = jax.random.split(jax.random.key(seed), 8)
    part_splits = jax.random.split(jax.random.fold_in(streams_of[7], part), 8)
    features = centred(part_splits[0], (NODES, HID), 1.0, 6.0, ((0, 16),))
    tile_values = centred(part_splits[1], (TILES, BLK, BLK), 0.028, 0.16992188, ((0, 16),))
    tile_rows = draw_tile_rows(jax.random.fold_in(jax.random.fold_in(streams_of[7], part), 71), part)
    tile_cols = draw_tile_cols(jax.random.fold_in(jax.random.fold_in(streams_of[7], part), 71), part)
    bias = centred(streams_of[4], (HID,), 0.5, 3.0, (), jnp.float32)
    weight = centred(streams_of[5], (HID, HID), HID ** -0.5, 0.375)
    cotangent = centred(part_splits[6], (NODES, HID), 1.0, 6.0, ((0, 16),))
    return dict(features=features, tile_values=tile_values, tile_rows=tile_rows, tile_cols=tile_cols, bias=bias, weight=weight, cotangent=cotangent)


def reference(features, tile_values, tile_rows, tile_cols, bias, weight, cotangent):
    nblk = NB_DEV * N_ROW
    xblocks = features.reshape(nblk, BLK, HID)
    tiles = tile_values.reshape(N_ROW, TILE_DEV, BLK, BLK)
    rows = tile_rows.reshape(N_ROW, TILE_DEV)
    cols = tile_cols.reshape(N_ROW, TILE_DEV)
    members = jnp.arange(NB_DEV, dtype=jnp.int32)

    def forward(items):
        tset, rset, cset = items
        blocks = xblocks[cset].astype(jnp.float32)
        prod = jnp.einsum('tab,tbh->tah', tset.astype(jnp.float32), blocks, precision=lax.Precision.HIGHEST)
        member = (rset[:, None] == members[None, :]).astype(jnp.float32)
        return jnp.einsum('tr,tah->rah', member, prod, precision=lax.Precision.HIGHEST)

    aggregate = lax.map(forward, (tiles, rows, cols)).reshape(NODES, HID).astype(jnp.bfloat16)
    preact = jnp.dot(aggregate, weight, preferred_element_type=jnp.float32) + bias
    hidden = jnp.maximum(preact, 0.0).astype(jnp.bfloat16)
    masked = jnp.where(preact > 0, cotangent, jnp.zeros_like(cotangent))
    grad_weight = jnp.dot(aggregate.T, masked, preferred_element_type=jnp.float32)
    grad_bias = jnp.sum(masked.astype(jnp.float32), axis=0)
    grad_agg = jnp.dot(masked, weight.T, preferred_element_type=jnp.float32).astype(jnp.bfloat16)
    panels = grad_agg.reshape(N_ROW, NB_DEV, BLK, HID)
    owners = jnp.arange(N_ROW, dtype=jnp.int32)

    def backward(carry, items):
        tset, rset, cset, panel, owner = items
        valid = rset >= 0
        source = panel[jnp.clip(rset, 0, NB_DEV - 1)].astype(jnp.float32)
        source = jnp.where(valid[:, None, None], source, jnp.zeros_like(source))
        contrib = jnp.einsum('tab,tah->tbh', tset.astype(jnp.float32), source, precision=lax.Precision.HIGHEST)
        relative = (cset - (owner - 1) * NB_DEV).astype(jnp.int32)
        local = jnp.zeros((3 * NB_DEV, BLK, HID), jnp.float32).at[relative].add(contrib)
        lower = local[:NB_DEV].astype(jnp.bfloat16)
        upper = local[2 * NB_DEV:].astype(jnp.bfloat16)
        lower, upper = lax.optimization_barrier((lower, upper))
        local = jnp.concatenate([lower.astype(jnp.float32), local[NB_DEV:2 * NB_DEV], upper.astype(jnp.float32)], axis=0)
        start = (owner * NB_DEV).astype(jnp.int32)
        zero = jnp.zeros((), jnp.int32)
        current = lax.dynamic_slice(carry, (start, zero, zero), (3 * NB_DEV, BLK, HID))
        carry = lax.dynamic_update_slice(carry, current + local, (start, zero, zero))
        return carry, None

    start_carry = jnp.zeros((nblk + 2 * NB_DEV, BLK, HID), jnp.float32)
    grad_x, unused = lax.scan(backward, start_carry, (tiles, rows, cols, panels, owners))
    grad_features = grad_x[NB_DEV:NB_DEV + nblk].reshape(NODES, HID).astype(jnp.bfloat16)
    return hidden, grad_features, grad_weight, grad_bias
```

```python
import functools

import jax
import jax.numpy as jnp
from jax import lax
from jax.experimental import pallas as pl
from jax.experimental.pallas import tpu as pltpu
from jax.sharding import PartitionSpec as P

MESH = pl.DeviceIdType.MESH
F32 = jnp.float32
BF16 = jnp.bfloat16


def stages_of(count):
    stages = []
    rest = count
    if rest % 2 == 0:
        stages.append((2, 1))
        rest //= 2
    low = count // rest
    while rest > 1:
        size = next(f for f in (4, 2, 3, 5, 7, rest) if rest % f == 0)
        rest //= size
        stages.append((size, low * rest))
    return stages


def splits_of(rows, stages):
    out = []
    for size, stride in stages:
        scatter = rows % (8 * size) == 0
        out.append((size, stride, rows, scatter))
        if scatter:
            rows //= size
    return out


def kernel(
    count, chunk, table, feat, tiles, bias, weight, cot,
    hid_out, gf_out, gw_out, gb_out,
    x, tv, pn, pt, adj, adj_lo, adjt, cv, g, hid, send, recv, own, gw, gwo, gb, rs_in, gb_in,
    local_sem, out_sem, halo_s, halo_r, part_s, part_r, rs_s, rs_r, gb_s, gb_r, ag_s, ag_r,
):
    me = lax.axis_index("row")
    rows, width = cv.shape
    slots, blk, _ = tv.shape
    nblk = rows // blk
    ncol = 3 * nblk
    stages = splits_of(gw.shape[0], stages_of(count))
    up, down = lax.rem(me + 1, count), lax.rem(me + count - 1, count)
    has_up, has_down = me < count - 1, me > 0

    def peer(size, stride, step):
        at = lax.rem(lax.div(me, stride), size)
        other = lax.rem(at + step, size)
        return at, other, me + (other - at) * stride

    cp_tiles = pltpu.make_async_copy(tiles, tv, local_sem.at[0])
    cp_feat = pltpu.make_async_copy(feat, x.at[1], local_sem.at[1])
    cp_cot = pltpu.make_async_copy(cot, cv, local_sem.at[2])
    cp_tiles.start()
    cp_feat.start()
    cp_cot.start()

    barrier = pltpu.get_barrier_semaphore()

    @pl.when(has_up)
    def _():
        pl.semaphore_signal(barrier, inc=1, device_id={"row": up}, device_id_type=MESH)

    @pl.when(has_down)
    def _():
        pl.semaphore_signal(barrier, inc=1, device_id={"row": down}, device_id_type=MESH)

    greeted = 0
    for size, stride, _, _ in stages:
        for step in range(1, size):
            _, _, dev = peer(size, stride, step)
            pl.semaphore_signal(barrier, inc=1, device_id={"row": dev}, device_id_type=MESH)
            greeted += 1
    pl.semaphore_wait(barrier, greeted + has_up.astype(jnp.int32) + has_down.astype(jnp.int32))

    halo_up = pltpu.make_async_remote_copy(
        feat, x.at[0], halo_s.at[0], halo_r.at[0], device_id={"row": up}, device_id_type=MESH)
    halo_down = pltpu.make_async_remote_copy(
        feat, x.at[2], halo_s.at[1], halo_r.at[1], device_id={"row": down}, device_id_type=MESH)

    @pl.when(has_up)
    def _():
        halo_up.start()

    @pl.when(has_down)
    def _():
        halo_down.start()

    @pl.when(jnp.logical_not(has_down))
    def _():
        x[0] = jnp.zeros((rows, width), BF16)
        recv[0] = jnp.zeros((rows, width), BF16)

    @pl.when(jnp.logical_not(has_up))
    def _():
        x[2] = jnp.zeros((rows, width), BF16)
        recv[1] = jnp.zeros((rows, width), BF16)

    pn[0] = jnp.zeros((blk, blk), F32)
    pt[0] = jnp.zeros((blk, blk), F32)
    cp_tiles.wait()

    def add_slot(s, carry):
        total = tv[s].astype(F32) + pn[table[s]]
        pn[s + 1] = total
        pt[s + 1] = total.T
        return carry

    lax.fori_loop(0, slots, add_slot, 0)

    def fill_row(r, carry):
        at = pl.multiple_of(r * blk, blk)
        for c in range(ncol):
            which = table[slots + r * ncol + c]
            cell = pn[which]
            top = cell.astype(BF16)
            adj[pl.ds(at, blk), c * blk:(c + 1) * blk] = top
            adj_lo[pl.ds(at, blk), c * blk:(c + 1) * blk] = (cell - top.astype(F32)).astype(BF16)
            adjt[c * blk:(c + 1) * blk, pl.ds(at, blk)] = pt[which].astype(BF16)
        return carry

    lax.fori_loop(0, nblk, fill_row, 0)

    cp_feat.wait()

    def strip(at, third):
        cols = slice(third * rows, (third + 1) * rows)
        return (jnp.dot(adj[at, cols], x[third], preferred_element_type=F32)
                + jnp.dot(adj_lo[at, cols], x[third], preferred_element_type=F32))

    def own_rows(i, carry):
        at = pl.ds(pl.multiple_of(i * chunk, chunk), chunk)
        own[at, :] = strip(at, 1)
        return carry

    lax.fori_loop(0, rows // chunk, own_rows, 0)

    cp_cot.wait()

    @pl.when(has_down)
    def _():
        halo_up.wait_recv()

    @pl.when(has_up)
    def _():
        halo_down.wait_recv()

    gw[...] = jnp.zeros_like(gw)
    gb[...] = jnp.zeros_like(gb)

    def dense(i, carry):
        at = pl.ds(pl.multiple_of(i * chunk, chunk), chunk)
        agg = (own[at, :] + strip(at, 0) + strip(at, 2)).astype(BF16)
        pre = jnp.dot(agg, weight[...], preferred_element_type=F32) + bias[...]
        hid[at, :] = jnp.maximum(pre, 0.0).astype(BF16)
        masked32 = jnp.where(pre > 0, cv[at, :].astype(F32), 0.0)
        masked = masked32.astype(BF16)
        gw[...] += lax.dot_general(agg, masked, (((0,), (0,)), ((), ())), preferred_element_type=F32)
        gb[...] += jnp.sum(masked32.reshape(chunk // 8, 8, width), axis=0)
        g[at, :] = lax.dot_general(
            masked, weight[...], (((1,), (1,)), ((), ())), preferred_element_type=F32).astype(BF16)
        return carry

    lax.fori_loop(0, rows // chunk, dense, 0)

    cp_hid = pltpu.make_async_copy(hid, hid_out, out_sem.at[0])
    cp_hid.start()

    bases = [0]
    plan = []
    first = 0
    for size, stride, n_rows, scatter in stages:
        plan.append((size, stride, n_rows // size if scatter else n_rows, scatter, first, bases[-1]))
        at = lax.rem(lax.div(me, stride), size)
        bases.append(bases[-1] + at * (n_rows // size) if scatter else bases[-1])
        first += size - 1

    def reduce_copies(k):
        size, stride, sub, scatter, first, base = plan[k]
        found = []
        for step in range(1, size):
            at, other, dev = peer(size, stride, step)
            sem = first + step - 1
            start = pl.multiple_of(base + other * sub, 8) if scatter else base
            found.append(pltpu.make_async_remote_copy(
                gw.at[pl.ds(start, sub)], rs_in.at[sem, pl.ds(0, sub)],
                rs_s.at[sem], rs_r.at[sem], device_id={"row": dev}, device_id_type=MESH))
            found.append(pltpu.make_async_remote_copy(
                gb.at[...], gb_in.at[sem],
                gb_s.at[sem], gb_r.at[sem], device_id={"row": dev}, device_id_type=MESH))
        return found

    def in_order(mine, slot, size, stride, first):
        at = lax.rem(lax.div(me, stride), size)
        total = None
        for member in range(size):
            term = jnp.where(at == member, mine, 0.0)
            for step in range(1, size):
                term = jnp.where(lax.rem(at - step + size, size) == member, slot(first + step - 1), term)
            total = term if total is None else total + term
        return total

    def reduce_finish(k, copies):
        size, stride, sub, scatter, first, base = plan[k]
        for c in copies:
            c.wait()
        start = pl.multiple_of(bases[k + 1], 8) if scatter else base
        here = pl.ds(start, sub)
        if scatter:
            total = gw[here, :]
            for step in range(1, size):
                total = total + rs_in[first + step - 1, :sub]
        else:
            total = in_order(gw[here, :], lambda i: rs_in[i, :sub], size, stride, first)
        gw[here, :] = total
        gb[...] = in_order(gb[...], lambda i: gb_in[i], size, stride, first)

    def gather_copies(k):
        size, stride, sub, scatter, first, base = plan[k]
        found = []
        if scatter:
            here = pl.ds(pl.multiple_of(bases[k + 1], 8), sub)
            for step in range(1, size):
                _, _, dev = peer(size, stride, step)
                sem = first + step - 1
                found.append(pltpu.make_async_remote_copy(
                    gwo.at[here], gwo.at[here],
                    ag_s.at[sem], ag_r.at[sem], device_id={"row": dev}, device_id_type=MESH))
        return found

    copies = reduce_copies(0)
    for c in copies:
        c.start()

    n_chunk = rows // chunk

    def part_copy(i, side):
        at = pl.ds(pl.multiple_of(i * chunk, chunk), chunk)
        return pltpu.make_async_remote_copy(
            send.at[side, at], recv.at[1 - side, at], part_s.at[side, i], part_r.at[side, i],
            device_id={"row": up if side else down}, device_id_type=MESH)

    def parts(i, carry):
        at = pl.multiple_of(i * chunk, chunk)
        for side, has in ((0, has_down), (1, has_up)):
            rows_at = pl.ds(pl.multiple_of(side * 2 * rows + at, chunk), chunk)
            send[side, pl.ds(at, chunk)] = jnp.dot(
                adjt[rows_at, :], g[...], preferred_element_type=F32).astype(BF16)

            @pl.when(has)
            def _():
                part_copy(i, side).start()
        return carry

    lax.fori_loop(0, n_chunk, parts, 0)

    reduce_finish(0, copies)
    if len(plan) > 1:
        copies = reduce_copies(1)
        for c in copies:
            c.start()

    def own_part(i, carry):
        at = pl.multiple_of(i * chunk, chunk)
        rows_at = pl.ds(pl.multiple_of(rows + at, chunk), chunk)
        own[pl.ds(at, chunk), :] = jnp.dot(adjt[rows_at, :], g[...], preferred_element_type=F32)
        return carry

    lax.fori_loop(0, n_chunk, own_part, 0)

    for k in range(1, len(plan)):
        reduce_finish(k, copies)
        if k + 1 < len(plan):
            copies = reduce_copies(k + 1)
            for c in copies:
                c.start()
    mine = pl.ds(pl.multiple_of(bases[-1], 8), plan[-1][2])
    gwo[mine, :] = gw[mine, :]
    cp_gb = pltpu.make_async_copy(gb, gb_out, out_sem.at[1])
    cp_gb.start()
    for k in reversed(range(len(plan))):
        copies = gather_copies(k)
        for c in copies:
            c.start()
        for c in copies:
            c.wait()
    cp_gw = pltpu.make_async_copy(gwo, gw_out, out_sem.at[2])
    cp_gw.start()

    cp_hid.wait()

    def finish(i, carry):
        at = pl.ds(pl.multiple_of(i * chunk, chunk), chunk)

        @pl.when(has_up)
        def _():
            part_copy(i, 0).wait_recv()

        @pl.when(has_down)
        def _():
            part_copy(i, 1).wait_recv()

        hid[at, :] = (own[at, :] + recv[0, at].astype(F32) + recv[1, at].astype(F32)).astype(BF16)
        return carry

    lax.fori_loop(0, n_chunk, finish, 0)
    cp_gf = pltpu.make_async_copy(hid, gf_out, out_sem.at[0])
    cp_gf.start()

    def sent(i, carry):
        @pl.when(has_down)
        def _():
            part_copy(i, 0).wait_send()

        @pl.when(has_up)
        def _():
            part_copy(i, 1).wait_send()
        return carry

    lax.fori_loop(0, n_chunk, sent, 0)

    @pl.when(has_up)
    def _():
        halo_up.wait_send()

    @pl.when(has_down)
    def _():
        halo_down.wait_send()

    cp_gf.wait()
    cp_gb.wait()
    cp_gw.wait()


def shards(count, features, tile_values, tile_rows, tile_cols, bias, weight, cotangent):
    slots, blk, _ = tile_values.shape
    rows, width = features.shape
    nblk = rows // blk
    ncol = 3 * nblk
    chunk = min(256, rows)
    rel = tile_cols - (lax.axis_index("row") - 1) * nblk
    key = jnp.where(tile_rows >= 0, tile_rows * ncol + rel, -1)
    wanted = jnp.concatenate([key, jnp.arange(nblk * ncol, dtype=jnp.int32)])
    limit = jnp.minimum(jnp.arange(slots + nblk * ncol, dtype=jnp.int32), slots)
    slot = jnp.arange(slots, dtype=jnp.int32)
    hit = (key[None, :] == wanted[:, None]) & (slot[None, :] < limit[:, None])
    table = jnp.max(jnp.where(hit, slot[None, :] + 1, 0), axis=1)

    stages = splits_of(width, stages_of(count))
    n_msg = max(1, sum(s[0] - 1 for s in stages))
    biggest = max([s[2] // s[0] if s[3] else s[2] for s in stages] + [8])
    hbm = pl.BlockSpec(memory_space=pl.ANY)
    vmem = pl.BlockSpec(memory_space=pltpu.VMEM)
    dma = pltpu.SemaphoreType.DMA
    hidden, grad_features, grad_weight, grad_bias = pl.pallas_call(
        functools.partial(kernel, count, chunk),
        out_shape=(
            jax.ShapeDtypeStruct((rows, width), BF16),
            jax.ShapeDtypeStruct((rows, width), BF16),
            jax.ShapeDtypeStruct((width, width), F32),
            jax.ShapeDtypeStruct((8, width), F32),
        ),
        in_specs=[pl.BlockSpec(memory_space=pltpu.SMEM), hbm, hbm, vmem, vmem, hbm],
        out_specs=(hbm, hbm, hbm, hbm),
        scratch_shapes=[
            pltpu.VMEM((3, rows, width), BF16),
            pltpu.VMEM((slots, blk, blk), BF16),
            pltpu.VMEM((slots + 1, blk, blk), F32),
            pltpu.VMEM((slots + 1, blk, blk), F32),
            pltpu.VMEM((rows, 3 * rows), BF16),
            pltpu.VMEM((rows, 3 * rows), BF16),
            pltpu.VMEM((3 * rows, rows), BF16),
            pltpu.VMEM((rows, width), BF16),
            pltpu.VMEM((rows, width), BF16),
            pltpu.VMEM((rows, width), BF16),
            pltpu.VMEM((2, rows, width), BF16),
            pltpu.VMEM((2, rows, width), BF16),
            pltpu.VMEM((rows, width), F32),
            pltpu.VMEM((width, width), F32),
            pltpu.VMEM((width, width), F32),
            pltpu.VMEM((8, width), F32),
            pltpu.VMEM((n_msg, biggest, width), F32),
            pltpu.VMEM((n_msg, 8, width), F32),
            dma((3,)),
            dma((3,)),
            dma((2,)),
            dma((2,)),
            dma((2, rows // chunk)),
            dma((2, rows // chunk)),
            dma((n_msg,)),
            dma((n_msg,)),
            dma((n_msg,)),
            dma((n_msg,)),
            dma((n_msg,)),
            dma((n_msg,)),
        ],
        compiler_params=pltpu.CompilerParams(
            collective_id=0, has_side_effects=True, vmem_limit_bytes=48 * 1024 * 1024),
    )(table, features, tile_values, bias.reshape(1, width), weight, cotangent)
    return hidden, grad_features, grad_weight, jnp.sum(grad_bias, axis=0)


def solution(mesh):
    return jax.shard_map(
        functools.partial(shards, mesh.shape["row"]),
        mesh=mesh,
        in_specs=(
            P(("groups", "row"), None),
            P(("groups", "row"), None, None),
            P(("groups", "row")),
            P(("groups", "row")),
            P(),
            P(),
            P(("groups", "row"), None),
        ),
        out_specs=(
            P(("groups", "row"), None),
            P(("groups", "row"), None),
            P("groups", None),
            P("groups"),
        ),
        check_vma=False,
    )
```
